32 devices in a mesh: grid: 8 (over z, x), cols: 4 (over y, core).
Axes of the slice: x: 2, y: 2, z: 4, core: 2. Of those that a mesh axis runs over, the one named last changes fastest.
Arguments:
- basis: float32 [1024, 3, 16, 1024], P('cols', None, 'grid'), may hold values from -1 to 1
- snapshots: float32 [128, 3, 16, 1024], P('cols', None, 'grid'), may hold values from -60 to 60
- permittivity: float32 [3, 16, 1024], P(None, 'grid'), may hold values from 1 to 10
- labels: int32 [16, 1024], P('grid'), may hold values from 0 to 7
- sigma_table: float32 [8], replicated, may hold values from 0.1 to 10
Outputs:
- new_basis: float32 [128, 3, 16, 1024], P('cols', None, 'grid')
- coefficients: float32 [1024, 128], P('cols')
- cross_terms: float32 [3, 1024, 128], P(None, 'cols')
- block_terms: float32 [3, 128, 128], P(None, 'cols')
The draws below stay inside these ranges and needn't reach their ends.
All inputs are finite; a program needn't handle non-finite values.
Results may differ from the reference program's by a relative error of at most 0.0003.
Values sent between devices are 32-bit elements; how exact they have to be, the bound alone decides.
A program may use at most 128 MiB of HBM per device.

```python
import math
import jax
import jax.numpy as jnp
from jax import lax

NX = 32
NY = 32
K = 1024
M = 128
NREG = 8
NZ = 16
NU = 49152


def basis_values(key):
    basis_key = jax.random.fold_in(key, 5)
    full_shape = (K, 3, NZ, NX * NY)
    values = jnp.clip(jax.random.normal(basis_key, full_shape, jnp.float32), -6.0, 6.0)
    return values * (1.0 / math.sqrt(NU))


def draw_basis(key, part):
    return basis_values(key).astype(jnp.float32)


def draw_snapshots(key, part):
    base_key = jax.random.fold_in(jax.random.fold_in(key, 11), 0)
    scale_key = jax.random.fold_in(jax.random.fold_in(key, 11), 1)
    mix_key = jax.random.fold_in(jax.random.fold_in(key, 11), 3)
    full_shape = (M, 3, NZ, NX * NY)
    basis_now = basis_values(key)
    depth_frac = jnp.arange(NZ, dtype=jnp.float32) / (NZ - 1)
    column_draw = jax.random.uniform(scale_key, (M, 1, 1, 1), jnp.float32)
    noise_level = math.sqrt(K / NU) / 25.0
    mixing = jnp.clip(jax.random.normal(mix_key, (K, M), jnp.float32), -6.0, 6.0)
    values = jnp.clip(jax.random.normal(base_key, full_shape, jnp.float32), -6.0, 6.0)
    depth_scale = 0.2157 * jnp.exp(math.log(10.0) * depth_frac)
    column_scale = 0.3 * jnp.exp(math.log(10.0) * column_draw)
    flat_basis = basis_now.reshape(K, -1)
    in_span = lax.dot_general(mixing, flat_basis, (((0,), (0,)), ((), ())), precision=lax.Precision.HIGHEST, preferred_element_type=jnp.float32)
    in_span = in_span.reshape(full_shape)
    noise_part = noise_level * values * depth_scale[None, None, :, None]
    return ((in_span + noise_part) * column_scale).astype(jnp.float32)


def with_ends(entries, rng, least, top_value):
    index_at = [jax.random.randint(jax.random.fold_in(rng, axis), (), 0, length) for axis, length in enumerate(entries.shape)]
    widest = entries.shape.index(max(entries.shape))
    beside = index_at[:widest] + [(index_at[widest] + 1) % entries.shape[widest]] + index_at[widest + 1:]
    return entries.at[tuple(index_at)].set(least).at[tuple(beside)].set(top_value)


def shard_levels(key, shape, cuts, low, top_value):
    level = 1.0
    for axis_at, parts in cuts:
        heights = jax.random.uniform(jax.random.fold_in(jax.random.fold_in(key, 6), axis_at), (parts,), jnp.float32, low / len(cuts), top_value / len(cuts))
        level = level * jnp.repeat(jnp.exp(heights), shape[axis_at] // parts).reshape((-1,) + (1,) * (len(shape) - 1 - axis_at))
    return level


def setup_inputs(seed: int = 0) -> dict:
    splits = jax.random.split(jax.random.key(seed), 6)
    basis = draw_basis(jax.random.fold_in(splits[5], 71), 0)
    snapshots = draw_snapshots(jax.random.fold_in(splits[5], 71), 0)
    permittivity = jnp.clip(jnp.exp(math.log(10.0) - 2.3025851 * jax.random.uniform(splits[2], (3, NZ, NX * NY), jnp.float32) ** shard_levels(splits[2], (3, NZ, NX * NY), ((1, 8),), -0.2, 0.2)), 1.0, 10.0)
    labels = with_ends(jax.random.randint(splits[3], (NZ, NX * NY), 0, NREG), jax.random.fold_in(splits[3], 1), 0, NREG - 1).astype(jnp.int32)
    sigma_table = jnp.clip(jnp.exp(jax.random.uniform(splits[4], (NREG,), jnp.float32, math.log(0.1), math.log(10.0))), 0.1, 10.0)
    return dict(basis=basis, snapshots=snapshots, permittivity=permittivity, labels=labels, sigma_table=sigma_table)


HIGHEST = lax.Precision.HIGHEST

def cells_dot(left_rows, right_rows):
    left_flat = left_rows.reshape(left_rows.shape[0], -1)
    right_flat = right_rows.reshape(right_rows.shape[0], -1)
    return lax.dot_general(left_flat.astype(jnp.float32), right_flat.astype(jnp.float32), (((1,), (1,)), ((), ())), precision=HIGHEST, preferred_element_type=jnp.float32)

def combine_rows(weights, fields):
    flattened = fields.reshape(fields.shape[0], -1)
    output_rows = lax.dot_general(weights.astype(jnp.float32), flattened.astype(jnp.float32), (((0,), (0,)), ((), ())), precision=HIGHEST, preferred_element_type=jnp.float32)
    return output_rows.reshape((weights.shape[1],) + fields.shape[1:])

def forward_x(field, row_len):
    padding_cols = jnp.zeros(field.shape[:-1] + (row_len,), field.dtype)
    return jnp.concatenate([field[..., row_len:], padding_cols], axis=-1)

def backward_x(field, row_len):
    padding_cols = jnp.zeros(field.shape[:-1] + (row_len,), field.dtype)
    return jnp.concatenate([padding_cols, field[..., :-row_len]], axis=-1)

def forward_y(field, row_len):
    column_pos = lax.broadcasted_iota(jnp.int32, (field.shape[-1],), 0) % row_len
    padding_cols = jnp.zeros(field.shape[:-1] + (1,), field.dtype)
    shifted = jnp.concatenate([field[..., 1:], padding_cols], axis=-1)
    return jnp.where(column_pos != row_len - 1, shifted, 0.0)

def backward_y(field, row_len):
    column_pos = lax.broadcasted_iota(jnp.int32, (field.shape[-1],), 0) % row_len
    padding_cols = jnp.zeros(field.shape[:-1] + (1,), field.dtype)
    shifted = jnp.concatenate([padding_cols, field[..., :-1]], axis=-1)
    return jnp.where(column_pos != 0, shifted, 0.0)

def curl_curl(extended, row_len):
    field_x = extended[:, 0]
    field_y = extended[:, 1]
    field_z = extended[:, 2]

    def middle(field):
        return field[:, 1:-1]

    def plus_x(field):
        return forward_x(field, row_len) - field

    def minus_x(field):
        return field - backward_x(field, row_len)

    def plus_y(field):
        return forward_y(field, row_len) - field

    def minus_y(field):
        return field - backward_y(field, row_len)

    def second_x(field):
        return forward_x(field, row_len) - 2.0 * field + backward_x(field, row_len)

    def second_y(field):
        return forward_y(field, row_len) - 2.0 * field + backward_y(field, row_len)

    def second_z(field):
        return field[:, 2:] - 2.0 * field[:, 1:-1] + field[:, :-2]
    curl_x = -second_y(middle(field_x)) - second_z(field_x) + minus_y(plus_x(middle(field_y))) + plus_x(middle(field_z)) - plus_x(field_z[:, :-2])
    curl_y = -second_x(middle(field_y)) - second_z(field_y) + minus_x(plus_y(middle(field_x))) + plus_y(middle(field_z)) - plus_y(field_z[:, :-2])
    curl_z = -second_x(middle(field_z)) - second_y(middle(field_z)) + minus_x(field_x[:, 2:] - middle(field_x)) + minus_y(field_y[:, 2:] - middle(field_y))
    return jnp.stack([curl_x, curl_y, curl_z], axis=1)

def lookup_sigma(labels, sigma_table):
    region_ids = jnp.arange(sigma_table.shape[0], dtype=jnp.int32)
    picked = jnp.where(labels[None] == region_ids[:, None, None], sigma_table[:, None, None], 0.0)
    return jnp.sum(picked, axis=0)

def reference(basis, snapshots, permittivity, labels, sigma_table):
    unknowns = 3 * NX * NY * NZ
    current = snapshots
    coefficients = jnp.zeros((basis.shape[0], snapshots.shape[0]), jnp.float32)
    for sweep_index in range(2):
        coef_part = cells_dot(basis, current)
        current = current - combine_rows(coef_part, basis)
        coefficients = coefficients + coef_part
    gram_sum = cells_dot(current, current) / unknowns
    lower_factor = jnp.linalg.cholesky(gram_sum)
    identity = jnp.eye(gram_sum.shape[0], dtype=jnp.float32)
    inverse = jax.scipy.linalg.solve_triangular(lower_factor, identity, lower=True)
    new_all = combine_rows(inverse.T, current)
    extended = jnp.pad(new_all, ((0, 0), (0, 0), (1, 1), (0, 0)))
    conductivity = lookup_sigma(labels, sigma_table)
    curl_term = curl_curl(extended, NY)
    mass_term = permittivity[None] * new_all
    loss_term = conductivity[None, None] * new_all
    cross_terms = jnp.stack([cells_dot(basis, curl_term), cells_dot(basis, mass_term), cells_dot(basis, loss_term)], axis=0)
    block_terms = jnp.stack([cells_dot(new_all, curl_term), cells_dot(new_all, mass_term), cells_dot(new_all, loss_term)], axis=0) / unknowns
    return (new_all, coefficients, cross_terms, block_terms)
```

```python
import functools

import jax
import jax.numpy as jnp
from jax import lax
from jax.experimental import pallas as pl
from jax.experimental.pallas import tpu as pltpu
from jax.sharding import PartitionSpec as P

NY = 32


HIGHEST = lax.Precision.HIGHEST
MESH = pl.DeviceIdType.MESH
STEP = 8


def cells_dot(left_rows, right_rows):
    left_flat = left_rows.reshape(left_rows.shape[0], -1)
    right_flat = right_rows.reshape(right_rows.shape[0], -1)
    return lax.dot_general(
        left_flat,
        right_flat,
        (((1,), (1,)), ((), ())),
        precision=HIGHEST,
        preferred_element_type=jnp.float32,
    )


def combine_rows(weights, fields):
    flattened = fields.reshape(fields.shape[0], -1)
    output_rows = lax.dot_general(
        weights,
        flattened,
        (((0,), (0,)), ((), ())),
        precision=HIGHEST,
        preferred_element_type=jnp.float32,
    )
    return output_rows.reshape((weights.shape[1],) + fields.shape[1:])


def forward_x(field, row_len):
    padding_cols = jnp.zeros(field.shape[:-1] + (row_len,), field.dtype)
    return jnp.concatenate([field[..., row_len:], padding_cols], axis=-1)


def backward_x(field, row_len):
    padding_cols = jnp.zeros(field.shape[:-1] + (row_len,), field.dtype)
    return jnp.concatenate([padding_cols, field[..., :-row_len]], axis=-1)


def forward_y(field, row_len):
    column_pos = lax.broadcasted_iota(jnp.int32, (field.shape[-1],), 0) % row_len
    padding_cols = jnp.zeros(field.shape[:-1] + (1,), field.dtype)
    shifted = jnp.concatenate([field[..., 1:], padding_cols], axis=-1)
    return jnp.where(column_pos != row_len - 1, shifted, 0.0)


def backward_y(field, row_len):
    column_pos = lax.broadcasted_iota(jnp.int32, (field.shape[-1],), 0) % row_len
    padding_cols = jnp.zeros(field.shape[:-1] + (1,), field.dtype)
    shifted = jnp.concatenate([padding_cols, field[..., :-1]], axis=-1)
    return jnp.where(column_pos != 0, shifted, 0.0)


def curl_curl(extended, row_len):
    field_x = extended[:, 0]
    field_y = extended[:, 1]
    field_z = extended[:, 2]

    def middle(field):
        return field[:, 1:-1]

    def plus_x(field):
        return forward_x(field, row_len) - field

    def minus_x(field):
        return field - backward_x(field, row_len)

    def plus_y(field):
        return forward_y(field, row_len) - field

    def minus_y(field):
        return field - backward_y(field, row_len)

    def second_x(field):
        return forward_x(field, row_len) - 2.0 * field + backward_x(field, row_len)

    def second_y(field):
        return forward_y(field, row_len) - 2.0 * field + backward_y(field, row_len)

    def second_z(field):
        return field[:, 2:] - 2.0 * field[:, 1:-1] + field[:, :-2]

    curl_x = (
        -second_y(middle(field_x))
        - second_z(field_x)
        + minus_y(plus_x(middle(field_y)))
        + plus_x(middle(field_z))
        - plus_x(field_z[:, :-2])
    )
    curl_y = (
        -second_x(middle(field_y))
        - second_z(field_y)
        + minus_x(plus_y(middle(field_x)))
        + plus_y(middle(field_z))
        - plus_y(field_z[:, :-2])
    )
    curl_z = (
        -second_x(middle(field_z))
        - second_y(middle(field_z))
        + minus_x(field_x[:, 2:] - middle(field_x))
        + minus_y(field_y[:, 2:] - middle(field_y))
    )
    return jnp.stack([curl_x, curl_y, curl_z], axis=1)


def lookup_sigma(labels, sigma_table):
    region_ids = jnp.arange(sigma_table.shape[0], dtype=jnp.int32)
    picked = jnp.where(labels[None] == region_ids[:, None, None], sigma_table[:, None, None], 0.0)
    return jnp.sum(picked, axis=0)


def rows_at(start, count):
    return pl.ds(pl.multiple_of(start, STEP), count)


def grid_sum_kernel(n, piece, x_ref, o_ref, slots, send_a, recv_a, send_b, recv_b):
    me = lax.axis_index("grid")
    col = lax.axis_index("cols")
    peers = [(lax.rem(me + k, n), col) for k in range(n)]
    barrier = pltpu.get_barrier_semaphore()
    for k in range(1, n):
        pl.semaphore_signal(barrier, inc=1, device_id=peers[k], device_id_type=MESH)
    pl.semaphore_wait(barrier, n - 1)
    scatter = {}
    for k in range(1, n):
        scatter[k] = pltpu.make_async_remote_copy(
            src_ref=x_ref.at[rows_at(peers[k][0] * piece, piece)],
            dst_ref=slots.at[k],
            send_sem=send_a.at[k],
            recv_sem=recv_a.at[k],
            device_id=peers[k],
            device_id_type=MESH,
        )
        scatter[k].start()
    mine = rows_at(me * piece, piece)
    total = x_ref[mine, :]
    for k in range(1, n):
        scatter[k].wait_recv()
        total = total + slots[k]
    o_ref[mine, :] = total
    spread = {}
    for k in range(1, n):
        spread[k] = pltpu.make_async_remote_copy(
            src_ref=o_ref.at[mine],
            dst_ref=o_ref.at[mine],
            send_sem=send_b.at[k],
            recv_sem=recv_b.at[k],
            device_id=peers[k],
            device_id_type=MESH,
        )
        spread[k].start()
    for k in range(1, n):
        spread[k].wait_recv()
    for k in range(1, n):
        scatter[k].wait_send()
        spread[k].wait_send()


def grid_sum(value, collective_id):
    n = lax.axis_size("grid")
    rows = value.shape[0]
    piece = -(-rows // (STEP * n)) * STEP
    padded_rows = piece * n
    if padded_rows != rows:
        value = jnp.pad(value, ((0, padded_rows - rows), (0, 0)))
    sems = [pltpu.SemaphoreType.DMA((n,))] * 4
    out = pl.pallas_call(
        functools.partial(grid_sum_kernel, n, piece),
        out_shape=jax.ShapeDtypeStruct(value.shape, jnp.float32),
        in_specs=[pl.BlockSpec(memory_space=pltpu.VMEM)],
        out_specs=pl.BlockSpec(memory_space=pltpu.VMEM),
        scratch_shapes=[pltpu.VMEM((n, piece, value.shape[1]), jnp.float32)] + sems,
        compiler_params=pltpu.CompilerParams(
            collective_id=collective_id, has_side_effects=True
        ),
    )(value)
    return out[:rows]


def chip_peers(chips):
    me = lax.axis_index("cols")
    grid = lax.axis_index("grid")
    chip, core = me // 2, lax.rem(me, 2)
    mate = (grid, chip * 2 + 1 - core)
    across = [(grid, lax.rem(chip + j, chips) * 2 + core) for j in range(chips)]
    return chip, core, mate, across


def chip_barrier(mate, across):
    barrier = pltpu.get_barrier_semaphore()
    for peer in [mate] + across[1:]:
        pl.semaphore_signal(barrier, inc=1, device_id=peer, device_id_type=MESH)
    pl.semaphore_wait(barrier, len(across))


def send(src, dst, sems, peer):
    copy = pltpu.make_async_remote_copy(
        src_ref=src,
        dst_ref=dst,
        send_sem=sems[0],
        recv_sem=sems[1],
        device_id=peer,
        device_id_type=MESH,
    )
    copy.start()
    return copy


def gather_kernel(chips, x_ref, o_ref, far_s, far_r, mate_s, mate_r):
    chip, core, mate, across = chip_peers(chips)
    rows = x_ref.shape[0]
    parts = rows // STEP
    chip_barrier(mate, across)
    far, near = {}, {}
    base = (chip * 2 + core) * rows
    for q in range(parts):
        for j in range(1, chips):
            far[j, q] = send(
                x_ref.at[pl.ds(q * STEP, STEP)],
                o_ref.at[rows_at(base + q * STEP, STEP)],
                (far_s.at[j, q], far_r.at[j, q]),
                across[j],
            )
    for q in range(parts):
        near[0, q] = send(
            x_ref.at[pl.ds(q * STEP, STEP)],
            o_ref.at[rows_at(base + q * STEP, STEP)],
            (mate_s.at[0, q], mate_r.at[0, q]),
            mate,
        )
    o_ref[rows_at(base, rows), :] = x_ref[...]
    for q in range(parts):
        for j in range(1, chips):
            far[j, q].wait_recv()
            origin = (lax.rem(chip + chips - j, chips) * 2 + core) * rows + q * STEP
            block = o_ref.at[rows_at(origin, STEP)]
            near[j, q] = send(block, block, (mate_s.at[j, q], mate_r.at[j, q]), mate)
    for copy in near.values():
        copy.wait_recv()
    for copy in list(near.values()) + list(far.values()):
        copy.wait_send()


def cols_gather(value, collective_id):
    n = lax.axis_size("cols")
    chips, parts = n // 2, value.shape[0] // STEP
    sems = [pltpu.SemaphoreType.DMA((chips, parts))] * 4
    return pl.pallas_call(
        functools.partial(gather_kernel, chips),
        out_shape=jax.ShapeDtypeStruct((n * value.shape[0], value.shape[1]), jnp.float32),
        in_specs=[pl.BlockSpec(memory_space=pltpu.VMEM)],
        out_specs=pl.BlockSpec(memory_space=pltpu.VMEM),
        scratch_shapes=sems,
        compiler_params=pltpu.CompilerParams(
            collective_id=collective_id, has_side_effects=True, vmem_limit_bytes=40 << 20
        ),
    )(value)


def project_kernel(
    chips, u_ref, s_ref, o_ref, from_mate, to_far, from_far,
    a_s, a_r, b_s, b_r, c_s, c_r, d_s, d_r,
):
    chip, core, mate, across = chip_peers(chips)
    half = u_ref.shape[0] // 2
    part = half // chips
    pieces = part // STEP
    chip_barrier(mate, across)
    order = list(range(1, chips)) + [0]
    index = [lax.rem(chip + j, chips) * part for j in range(chips)]
    first, second, third, fourth = {}, {}, {}, {}
    for j in order:
        for q in range(pieces):
            first[j, q] = send(
                u_ref.at[rows_at((1 - core) * half + index[j] + q * STEP, STEP)],
                from_mate.at[j, q],
                (a_s.at[j, q], a_r.at[j, q]),
                mate,
            )
    for q in range(pieces):
        for j in range(1, chips):
            first[j, q].wait_recv()
            to_far[j, q] = u_ref[rows_at(core * half + index[j] + q * STEP, STEP), :] + from_mate[j, q]
            second[j, q] = send(
                to_far.at[j, q], from_far.at[j, q], (b_s.at[j, q], b_r.at[j, q]), across[j]
            )
    for q in range(pieces):
        mine = rows_at(core * half + index[0] + q * STEP, STEP)
        first[0, q].wait_recv()
        total = u_ref[mine, :] + from_mate[0, q]
        for j in range(1, chips):
            second[j, q].wait_recv()
            total = total + from_far[j, q]
        o_ref[mine, :] = s_ref[mine, :] - total
        for j in range(1, chips):
            third[j, q] = send(
                o_ref.at[mine], o_ref.at[mine], (c_s.at[j, q], c_r.at[j, q]), across[j]
            )
        fourth[0, q] = send(
            o_ref.at[mine], o_ref.at[mine], (d_s.at[0, q], d_r.at[0, q]), mate
        )
    for q in range(pieces):
        for j in range(1, chips):
            third[j, q].wait_recv()
            origin = core * half + lax.rem(chip + chips - j, chips) * part + q * STEP
            block = o_ref.at[rows_at(origin, STEP)]
            fourth[j, q] = send(block, block, (d_s.at[j, q], d_r.at[j, q]), mate)
    for copy in fourth.values():
        copy.wait_recv()
    for group in (first, second, third, fourth):
        for copy in group.values():
            copy.wait_send()


def project(combined, current, collective_id):
    chips = lax.axis_size("cols") // 2
    rows, width = combined.shape
    pieces = rows // 2 // chips // STEP
    slot = pltpu.VMEM((chips, pieces, STEP, width), jnp.float32)
    return pl.pallas_call(
        functools.partial(project_kernel, chips),
        out_shape=jax.ShapeDtypeStruct(combined.shape, jnp.float32),
        in_specs=[pl.BlockSpec(memory_space=pltpu.VMEM)] * 2,
        out_specs=pl.BlockSpec(memory_space=pltpu.VMEM),
        scratch_shapes=[slot] * 3 + [pltpu.SemaphoreType.DMA((chips, pieces))] * 8,
        compiler_params=pltpu.CompilerParams(
            collective_id=collective_id, has_side_effects=True, vmem_limit_bytes=40 << 20
        ),
    )(combined, current)


def shards(basis, snapshots, permittivity, labels, sigma_table):
    snap_cols = snapshots.shape[0]
    basis_cols = basis.shape[0]
    cell_shape = basis.shape[1:]
    grid_size = lax.axis_size("grid")
    total_snap = snap_cols * lax.axis_size("cols")
    unknowns = 3 * snapshots.shape[3] * snapshots.shape[2] * grid_size
    conductivity = lookup_sigma(labels, sigma_table)
    flat_basis = basis.reshape(basis_cols, -1)
    current = cols_gather(snapshots.reshape(snap_cols, -1), 1)
    coefficients = None
    for sweep_index in range(2):
        coef_part = grid_sum(cells_dot(flat_basis, current), 2 + sweep_index)
        current = project(combine_rows(coef_part, flat_basis), current, 4 + sweep_index)
        coefficients = coef_part if coefficients is None else coefficients + coef_part
    finished = current.reshape((total_snap,) + cell_shape)
    up = [(i, i + 1) for i in range(grid_size - 1)]
    down = [(j, i) for i, j in up]
    below = lax.ppermute(finished[:, :, -1:], "grid", up)
    above = lax.ppermute(finished[:, :2, :1], "grid", down)
    gram_sum = grid_sum(cells_dot(current, current), 6) / unknowns
    lower_factor = jnp.linalg.cholesky(gram_sum)
    identity = jnp.eye(total_snap, dtype=jnp.float32)
    inverse = jax.scipy.linalg.solve_triangular(lower_factor, identity, lower=True)
    own_start = lax.axis_index("cols") * snap_cols
    new_all = combine_rows(inverse.T, finished)
    new_below = combine_rows(inverse.T, below)
    new_above = combine_rows(inverse.T, above)
    new_above = jnp.concatenate([new_above, jnp.zeros_like(new_above[:, :1])], axis=1)
    extended = jnp.concatenate([new_below, new_all, new_above], axis=2)
    curl_term = curl_curl(extended, NY)
    mass_term = permittivity[None] * new_all
    loss_term = conductivity[None, None] * new_all
    own_new = lax.dynamic_slice_in_dim(new_all, own_start, snap_cols, 0)
    own_flat = own_new.reshape(snap_cols, -1)
    pieces = []
    for term in (curl_term, mass_term, loss_term):
        pieces.append(cells_dot(flat_basis, term))
    for term in (curl_term, mass_term, loss_term):
        pieces.append(cells_dot(own_flat, term) / unknowns)
    terms = grid_sum(jnp.concatenate(pieces, axis=0), 7)
    cut = 3 * basis_cols
    cross_terms = terms[:cut].reshape(3, basis_cols, total_snap)
    block_terms = terms[cut:].reshape(3, snap_cols, total_snap)
    return (own_new, coefficients, cross_terms, block_terms)


def solution(mesh):
    placed = (
        P("cols", None, "grid", None),
        P("cols", None, "grid", None),
        P(None, "grid", None),
        P("grid", None),
        P(),
    )
    return jax.shard_map(
        shards,
        mesh=mesh,
        in_specs=placed,
        out_specs=(
            P("cols", None, "grid", None),
            P("cols", None),
            P(None, "cols", None),
            P(None, "cols", None),
        ),
        check_vma=False,
    )
```

```python
import functools

import jax
import jax.numpy as jnp
from jax import lax
from jax.experimental import pallas as pl
from jax.experimental.pallas import tpu as pltpu
from jax.sharding import PartitionSpec as P

NY = 32


HIGHEST = lax.Precision.HIGHEST
HIGH = lax.Precision.HIGH
MESH = pl.DeviceIdType.MESH
STEP = 8


def cells_dot(left_rows, right_rows, precision=HIGH):
    left_flat = left_rows.reshape(left_rows.shape[0], -1)
    right_flat = right_rows.reshape(right_rows.shape[0], -1)
    return lax.dot_general(
        left_flat,
        right_flat,
        (((1,), (1,)), ((), ())),
        precision=precision,
        preferred_element_type=jnp.float32,
    )


def combine_rows(weights, fields, precision=HIGH):
    flattened = fields.reshape(fields.shape[0], -1)
    output_rows = lax.dot_general(
        weights,
        flattened,
        (((0,), (0,)), ((), ())),
        precision=precision,
        preferred_element_type=jnp.float32,
    )
    return output_rows.reshape((weights.shape[1],) + fields.shape[1:])


def forward_x(field, row_len):
    padding_cols = jnp.zeros(field.shape[:-1] + (row_len,), field.dtype)
    return jnp.concatenate([field[..., row_len:], padding_cols], axis=-1)


def backward_x(field, row_len):
    padding_cols = jnp.zeros(field.shape[:-1] + (row_len,), field.dtype)
    return jnp.concatenate([padding_cols, field[..., :-row_len]], axis=-1)


def forward_y(field, row_len):
    column_pos = lax.broadcasted_iota(jnp.int32, (field.shape[-1],), 0) % row_len
    padding_cols = jnp.zeros(field.shape[:-1] + (1,), field.dtype)
    shifted = jnp.concatenate([field[..., 1:], padding_cols], axis=-1)
    return jnp.where(column_pos != row_len - 1, shifted, 0.0)


def backward_y(field, row_len):
    column_pos = lax.broadcasted_iota(jnp.int32, (field.shape[-1],), 0) % row_len
    padding_cols = jnp.zeros(field.shape[:-1] + (1,), field.dtype)
    shifted = jnp.concatenate([padding_cols, field[..., :-1]], axis=-1)
    return jnp.where(column_pos != 0, shifted, 0.0)


def curl_curl(field_x, field_y, field_z, row_len):
    def plus_x(field):
        return forward_x(field, row_len) - field

    def minus_x(field):
        return field - backward_x(field, row_len)

    def plus_y(field):
        return forward_y(field, row_len) - field

    def minus_y(field):
        return field - backward_y(field, row_len)

    def second_x(field):
        return forward_x(field, row_len) - 2.0 * field + backward_x(field, row_len)

    def second_y(field):
        return forward_y(field, row_len) - 2.0 * field + backward_y(field, row_len)

    images = ([], [], [])
    for at in range(1, len(field_x) - 1):
        x_low, x_mid, x_top = field_x[at - 1 : at + 2]
        y_low, y_mid, y_top = field_y[at - 1 : at + 2]
        z_low, z_mid = field_z[at - 1 : at + 1]
        images[0].append(
            -second_y(x_mid)
            - (x_top - 2.0 * x_mid + x_low)
            + minus_y(plus_x(y_mid))
            + plus_x(z_mid - z_low)
        )
        images[1].append(
            -second_x(y_mid)
            - (y_top - 2.0 * y_mid + y_low)
            + minus_x(plus_y(x_mid))
            + plus_y(z_mid - z_low)
        )
        images[2].append(
            -second_x(z_mid) - second_y(z_mid) + minus_x(x_top - x_mid) + minus_y(y_top - y_mid)
        )
    return jnp.concatenate(images[0] + images[1] + images[2], axis=-1)


def lookup_sigma(labels, sigma_table):
    region_ids = jnp.arange(sigma_table.shape[0], dtype=jnp.int32)
    picked = jnp.where(labels[None] == region_ids[:, None, None], sigma_table[:, None, None], 0.0)
    return jnp.sum(picked, axis=0)


def rows_at(start, count):
    return pl.ds(pl.multiple_of(start, STEP), count)


def grid_sum_kernel(n, piece, x_ref, o_ref, slots, send_a, recv_a, send_b, recv_b):
    me = lax.axis_index("grid")
    col = lax.axis_index("cols")
    peers = [(lax.rem(me + k, n), col) for k in range(n)]
    barrier = pltpu.get_barrier_semaphore()
    for k in range(1, n):
        pl.semaphore_signal(barrier, inc=1, device_id=peers[k], device_id_type=MESH)
    pl.semaphore_wait(barrier, n - 1)
    scatter = {}
    for k in range(1, n):
        scatter[k] = pltpu.make_async_remote_copy(
            src_ref=x_ref.at[rows_at(peers[k][0] * piece, piece)],
            dst_ref=slots.at[k],
            send_sem=send_a.at[k],
            recv_sem=recv_a.at[k],
            device_id=peers[k],
            device_id_type=MESH,
        )
        scatter[k].start()
    mine = rows_at(me * piece, piece)
    total = x_ref[mine, :]
    for k in range(1, n):
        scatter[k].wait_recv()
        total = total + slots[k]
    o_ref[mine, :] = total
    spread = {}
    for k in range(1, n):
        spread[k] = pltpu.make_async_remote_copy(
            src_ref=o_ref.at[mine],
            dst_ref=o_ref.at[mine],
            send_sem=send_b.at[k],
            recv_sem=recv_b.at[k],
            device_id=peers[k],
            device_id_type=MESH,
        )
        spread[k].start()
    for k in range(1, n):
        spread[k].wait_recv()
    for k in range(1, n):
        scatter[k].wait_send()
        spread[k].wait_send()


def grid_sum(value, collective_id):
    n = lax.axis_size("grid")
    rows = value.shape[0]
    piece = -(-rows // (STEP * n)) * STEP
    padded_rows = piece * n
    if padded_rows != rows:
        value = jnp.pad(value, ((0, padded_rows - rows), (0, 0)))
    sems = [pltpu.SemaphoreType.DMA((n,))] * 4
    out = pl.pallas_call(
        functools.partial(grid_sum_kernel, n, piece),
        out_shape=jax.ShapeDtypeStruct(value.shape, jnp.float32),
        in_specs=[pl.BlockSpec(memory_space=pltpu.VMEM)],
        out_specs=pl.BlockSpec(memory_space=pltpu.VMEM),
        scratch_shapes=[pltpu.VMEM((n, piece, value.shape[1]), jnp.float32)] + sems,
        compiler_params=pltpu.CompilerParams(
            collective_id=collective_id, has_side_effects=True
        ),
    )(value)
    return out[:rows]


def chip_peers(chips):
    me = lax.axis_index("cols")
    grid = lax.axis_index("grid")
    chip, core = me // 2, lax.rem(me, 2)
    mate = (grid, chip * 2 + 1 - core)
    across = [(grid, lax.rem(chip + j, chips) * 2 + core) for j in range(chips)]
    return chip, core, mate, across


def chip_barrier(mate, across):
    barrier = pltpu.get_barrier_semaphore()
    for peer in [mate] + across[1:]:
        pl.semaphore_signal(barrier, inc=1, device_id=peer, device_id_type=MESH)
    pl.semaphore_wait(barrier, len(across))


def send(src, dst, sems, peer):
    copy = pltpu.make_async_remote_copy(
        src_ref=src,
        dst_ref=dst,
        send_sem=sems[0],
        recv_sem=sems[1],
        device_id=peer,
        device_id_type=MESH,
    )
    copy.start()
    return copy


def gather_kernel(chips, x_ref, o_ref, far_s, far_r, mate_s, mate_r):
    chip, core, mate, across = chip_peers(chips)
    rows = x_ref.shape[0]
    parts = rows // STEP
    chip_barrier(mate, across)
    far, near = {}, {}
    base = (chip * 2 + core) * rows
    for q in range(parts):
        for j in range(1, chips):
            far[j, q] = send(
                x_ref.at[pl.ds(q * STEP, STEP)],
                o_ref.at[rows_at(base + q * STEP, STEP)],
                (far_s.at[j, q], far_r.at[j, q]),
                across[j],
            )
    for q in range(parts):
        near[0, q] = send(
            x_ref.at[pl.ds(q * STEP, STEP)],
            o_ref.at[rows_at(base + q * STEP, STEP)],
            (mate_s.at[0, q], mate_r.at[0, q]),
            mate,
        )
    o_ref[rows_at(base, rows), :] = x_ref[...]
    for q in range(parts):
        for j in range(1, chips):
            far[j, q].wait_recv()
            origin = (lax.rem(chip + chips - j, chips) * 2 + core) * rows + q * STEP
            block = o_ref.at[rows_at(origin, STEP)]
            near[j, q] = send(block, block, (mate_s.at[j, q], mate_r.at[j, q]), mate)
    for copy in near.values():
        copy.wait_recv()
    for copy in list(near.values()) + list(far.values()):
        copy.wait_send()


def cols_gather(value, collective_id):
    n = lax.axis_size("cols")
    chips, parts = n // 2, value.shape[0] // STEP
    sems = [pltpu.SemaphoreType.DMA((chips, parts))] * 4
    return pl.pallas_call(
        functools.partial(gather_kernel, chips),
        out_shape=jax.ShapeDtypeStruct((n * value.shape[0], value.shape[1]), jnp.float32),
        in_specs=[pl.BlockSpec(memory_space=pltpu.VMEM)],
        out_specs=pl.BlockSpec(memory_space=pltpu.VMEM),
        scratch_shapes=sems,
        compiler_params=pltpu.CompilerParams(
            collective_id=collective_id, has_side_effects=True, vmem_limit_bytes=40 << 20
        ),
    )(value)


def project_kernel(
    chips, u_ref, s_ref, o_ref, from_mate, to_far, from_far,
    a_s, a_r, b_s, b_r, c_s, c_r, d_s, d_r,
):
    chip, core, mate, across = chip_peers(chips)
    half = u_ref.shape[0] // 2
    part = half // chips
    pieces = part // STEP
    chip_barrier(mate, across)
    order = list(range(1, chips)) + [0]
    index = [lax.rem(chip + j, chips) * part for j in range(chips)]
    first, second, third, fourth = {}, {}, {}, {}
    for j in order:
        for q in range(pieces):
            first[j, q] = send(
                u_ref.at[rows_at((1 - core) * half + index[j] + q * STEP, STEP)],
                from_mate.at[j, q],
                (a_s.at[j, q], a_r.at[j, q]),
                mate,
            )
    for q in range(pieces):
        for j in range(1, chips):
            first[j, q].wait_recv()
            to_far[j, q] = u_ref[rows_at(core * half + index[j] + q * STEP, STEP), :] + from_mate[j, q]
            second[j, q] = send(
                to_far.at[j, q], from_far.at[j, q], (b_s.at[j, q], b_r.at[j, q]), across[j]
            )
    for q in range(pieces):
        mine = rows_at(core * half + index[0] + q * STEP, STEP)
        first[0, q].wait_recv()
        total = u_ref[mine, :] + from_mate[0, q]
        for j in range(1, chips):
            second[j, q].wait_recv()
            total = total + from_far[j, q]
        o_ref[mine, :] = s_ref[mine, :] - total
        for j in range(1, chips):
            third[j, q] = send(
                o_ref.at[mine], o_ref.at[mine], (c_s.at[j, q], c_r.at[j, q]), across[j]
            )
        fourth[0, q] = send(
            o_ref.at[mine], o_ref.at[mine], (d_s.at[0, q], d_r.at[0, q]), mate
        )
    for q in range(pieces):
        for j in range(1, chips):
            third[j, q].wait_recv()
            origin = core * half + lax.rem(chip + chips - j, chips) * part + q * STEP
            block = o_ref.at[rows_at(origin, STEP)]
            fourth[j, q] = send(block, block, (d_s.at[j, q], d_r.at[j, q]), mate)
    for copy in fourth.values():
        copy.wait_recv()
    for group in (first, second, third, fourth):
        for copy in group.values():
            copy.wait_send()


def project(combined, current, collective_id):
    chips = lax.axis_size("cols") // 2
    rows, width = combined.shape
    pieces = rows // 2 // chips // STEP
    slot = pltpu.VMEM((chips, pieces, STEP, width), jnp.float32)
    return pl.pallas_call(
        functools.partial(project_kernel, chips),
        out_shape=jax.ShapeDtypeStruct(combined.shape, jnp.float32),
        in_specs=[pl.BlockSpec(memory_space=pltpu.VMEM)] * 2,
        out_specs=pl.BlockSpec(memory_space=pltpu.VMEM),
        scratch_shapes=[slot] * 3 + [pltpu.SemaphoreType.DMA((chips, pieces))] * 8,
        compiler_params=pltpu.CompilerParams(
            collective_id=collective_id, has_side_effects=True, vmem_limit_bytes=40 << 20
        ),
    )(combined, current)


def shards(basis, snapshots, permittivity, labels, sigma_table):
    snap_cols = snapshots.shape[0]
    basis_cols = basis.shape[0]
    cell_shape = basis.shape[1:]
    grid_size = lax.axis_size("grid")
    total_snap = snap_cols * lax.axis_size("cols")
    unknowns = 3 * snapshots.shape[3] * snapshots.shape[2] * grid_size
    conductivity = lookup_sigma(labels, sigma_table)
    flat_basis = basis.reshape(basis_cols, -1)
    current = cols_gather(snapshots.reshape(snap_cols, -1), 1)
    coefficients = None
    for sweep_index in range(2):
        coef_part = grid_sum(cells_dot(flat_basis, current), 2 + sweep_index)
        combined = combine_rows(coef_part, flat_basis, HIGH if sweep_index else HIGHEST)
        current = project(combined, current, 4 + sweep_index)
        coefficients = coef_part if coefficients is None else coefficients + coef_part
    layers, layer = cell_shape[1], cell_shape[2]

    def layer_of(fields, component, at, count):
        start = (component * count + at) * layer
        return fields[:, start : start + layer]

    gram_sum = grid_sum(cells_dot(current, current), 6) / unknowns
    top = jnp.concatenate([layer_of(current, a, layers - 1, layers) for a in range(3)], axis=1)
    bottom = jnp.concatenate([layer_of(current, a, 0, layers) for a in range(2)], axis=1)
    gram_sum, top, bottom = lax.optimization_barrier((gram_sum, top, bottom))
    up = [(i, i + 1) for i in range(grid_size - 1)]
    down = [(j, i) for i, j in up]
    below = lax.ppermute(top, "grid", up)
    above = lax.ppermute(bottom, "grid", down)
    lower_factor = jnp.linalg.cholesky(gram_sum)
    identity = jnp.eye(total_snap, dtype=jnp.float32)
    inverse = jax.scipy.linalg.solve_triangular(lower_factor, identity, lower=True).T
    own_start = lax.axis_index("cols") * snap_cols
    new_all = combine_rows(inverse, current)
    mass_term = permittivity.reshape(1, -1) * new_all
    loss_term = jnp.tile(conductivity.reshape(1, -1), (1, 3)) * new_all
    own_flat = lax.dynamic_slice_in_dim(new_all, own_start, snap_cols, 0)
    own_new = own_flat.reshape(snapshots.shape)
    new_below = combine_rows(inverse, below)
    new_above = combine_rows(inverse, above)
    extended = []
    for a in range(3):
        column = [layer_of(new_below, a, 0, 1)]
        column += [layer_of(new_all, a, at, layers) for at in range(layers)]
        if a < 2:
            column.append(layer_of(new_above, a, 0, 1))
        extended.append(column)
    curl_term = curl_curl(*extended, NY)
    pieces = [
        cells_dot(flat_basis, mass_term),
        cells_dot(flat_basis, loss_term),
        cells_dot(own_flat, mass_term) / unknowns,
        cells_dot(own_flat, loss_term) / unknowns,
        cells_dot(flat_basis, curl_term),
        cells_dot(own_flat, curl_term) / unknowns,
    ]
    terms = grid_sum(jnp.concatenate(pieces, axis=0), 7)
    starts = [0]
    for piece in pieces:
        starts.append(starts[-1] + piece.shape[0])
    parts = [terms[low:high] for low, high in zip(starts[:-1], starts[1:])]
    cross_terms = jnp.stack([parts[4], parts[0], parts[1]])
    block_terms = jnp.stack([parts[5], parts[2], parts[3]])
    return (own_new, coefficients, cross_terms, block_terms)


def solution(mesh):
    placed = (
        P("cols", None, "grid", None),
        P("cols", None, "grid", None),
        P(None, "grid", None),
        P("grid", None),
        P(),
    )
    return jax.shard_map(
        shards,
        mesh=mesh,
        in_specs=placed,
        out_specs=(
            P("cols", None, "grid", None),
            P("cols", None),
            P(None, "cols", None),
            P(None, "cols", None),
        ),
        check_vma=False,
    )
```

```python
import functools

import jax
import jax.numpy as jnp
from jax import lax
from jax.experimental import pallas as pl
from jax.experimental.pallas import tpu as pltpu
from jax.sharding import PartitionSpec as P

NY = 32


HIGHEST = lax.Precision.HIGHEST
HIGH = lax.Precision.HIGH
MESH = pl.DeviceIdType.MESH
STEP = 8


def cells_dot(left_rows, right_rows, precision=HIGH):
    left_flat = left_rows.reshape(left_rows.shape[0], -1)
    right_flat = right_rows.reshape(right_rows.shape[0], -1)
    return lax.dot_general(
        left_flat,
        right_flat,
        (((1,), (1,)), ((), ())),
        precision=precision,
        preferred_element_type=jnp.float32,
    )


def combine_rows(weights, fields, precision=HIGH):
    flattened = fields.reshape(fields.shape[0], -1)
    output_rows = lax.dot_general(
        weights,
        flattened,
        (((0,), (0,)), ((), ())),
        precision=precision,
        preferred_element_type=jnp.float32,
    )
    return output_rows.reshape((weights.shape[1],) + fields.shape[1:])


def forward_x(field, row_len):
    padding_cols = jnp.zeros(field.shape[:-1] + (row_len,), field.dtype)
    return jnp.concatenate([field[..., row_len:], padding_cols], axis=-1)


def backward_x(field, row_len):
    padding_cols = jnp.zeros(field.shape[:-1] + (row_len,), field.dtype)
    return jnp.concatenate([padding_cols, field[..., :-row_len]], axis=-1)


def forward_y(field, row_len):
    column_pos = lax.broadcasted_iota(jnp.int32, (field.shape[-1],), 0) % row_len
    padding_cols = jnp.zeros(field.shape[:-1] + (1,), field.dtype)
    shifted = jnp.concatenate([field[..., 1:], padding_cols], axis=-1)
    return jnp.where(column_pos != row_len - 1, shifted, 0.0)


def backward_y(field, row_len):
    column_pos = lax.broadcasted_iota(jnp.int32, (field.shape[-1],), 0) % row_len
    padding_cols = jnp.zeros(field.shape[:-1] + (1,), field.dtype)
    shifted = jnp.concatenate([padding_cols, field[..., :-1]], axis=-1)
    return jnp.where(column_pos != 0, shifted, 0.0)


def curl_curl(field_x, field_y, field_z, row_len):
    def plus_x(field):
        return forward_x(field, row_len) - field

    def minus_x(field):
        return field - backward_x(field, row_len)

    def plus_y(field):
        return forward_y(field, row_len) - field

    def minus_y(field):
        return field - backward_y(field, row_len)

    def second_x(field):
        return forward_x(field, row_len) - 2.0 * field + backward_x(field, row_len)

    def second_y(field):
        return forward_y(field, row_len) - 2.0 * field + backward_y(field, row_len)

    images = ([], [], [])
    for at in range(1, len(field_x) - 1):
        x_low, x_mid, x_top = field_x[at - 1 : at + 2]
        y_low, y_mid, y_top = field_y[at - 1 : at + 2]
        z_low, z_mid = field_z[at - 1 : at + 1]
        images[0].append(
            -second_y(x_mid)
            - (x_top - 2.0 * x_mid + x_low)
            + minus_y(plus_x(y_mid))
            + plus_x(z_mid - z_low)
        )
        images[1].append(
            -second_x(y_mid)
            - (y_top - 2.0 * y_mid + y_low)
            + minus_x(plus_y(x_mid))
            + plus_y(z_mid - z_low)
        )
        images[2].append(
            -second_x(z_mid) - second_y(z_mid) + minus_x(x_top - x_mid) + minus_y(y_top - y_mid)
        )
    return jnp.concatenate(images[0] + images[1] + images[2], axis=-1)


def lookup_sigma(labels, sigma_table):
    region_ids = jnp.arange(sigma_table.shape[0], dtype=jnp.int32)
    picked = jnp.where(labels[None] == region_ids[:, None, None], sigma_table[:, None, None], 0.0)
    return jnp.sum(picked, axis=0)


def rows_at(start, count):
    return pl.ds(pl.multiple_of(start, STEP), count)


def grid_sum_kernel(n, piece, x_ref, o_ref, slots, send_a, recv_a, send_b, recv_b):
    me = lax.axis_index("grid")
    col = lax.axis_index("cols")
    peers = [(lax.rem(me + k, n), col) for k in range(n)]
    barrier = pltpu.get_barrier_semaphore()
    for k in range(1, n):
        pl.semaphore_signal(barrier, inc=1, device_id=peers[k], device_id_type=MESH)
    pl.semaphore_wait(barrier, n - 1)
    scatter = {}
    for k in range(1, n):
        scatter[k] = pltpu.make_async_remote_copy(
            src_ref=x_ref.at[rows_at(peers[k][0] * piece, piece)],
            dst_ref=slots.at[k],
            send_sem=send_a.at[k],
            recv_sem=recv_a.at[k],
            device_id=peers[k],
            device_id_type=MESH,
        )
        scatter[k].start()
    mine = rows_at(me * piece, piece)
    total = x_ref[mine, :]
    for k in range(1, n):
        scatter[k].wait_recv()
        total = total + slots[k]
    o_ref[mine, :] = total
    spread = {}
    for k in range(1, n):
        spread[k] = pltpu.make_async_remote_copy(
            src_ref=o_ref.at[mine],
            dst_ref=o_ref.at[mine],
            send_sem=send_b.at[k],
            recv_sem=recv_b.at[k],
            device_id=peers[k],
            device_id_type=MESH,
        )
        spread[k].start()
    for k in range(1, n):
        spread[k].wait_recv()
    for k in range(1, n):
        scatter[k].wait_send()
        spread[k].wait_send()


def grid_sum(value, collective_id):
    n = lax.axis_size("grid")
    rows = value.shape[0]
    piece = -(-rows // (STEP * n)) * STEP
    padded_rows = piece * n
    if padded_rows != rows:
        value = jnp.pad(value, ((0, padded_rows - rows), (0, 0)))
    sems = [pltpu.SemaphoreType.DMA((n,))] * 4
    out = pl.pallas_call(
        functools.partial(grid_sum_kernel, n, piece),
        out_shape=jax.ShapeDtypeStruct(value.shape, jnp.float32),
        in_specs=[pl.BlockSpec(memory_space=pltpu.VMEM)],
        out_specs=pl.BlockSpec(memory_space=pltpu.VMEM),
        scratch_shapes=[pltpu.VMEM((n, piece, value.shape[1]), jnp.float32)] + sems,
        compiler_params=pltpu.CompilerParams(
            collective_id=collective_id, has_side_effects=True
        ),
    )(value)
    return out[:rows]


def chip_peers(chips):
    me = lax.axis_index("cols")
    grid = lax.axis_index("grid")
    chip, core = me // 2, lax.rem(me, 2)
    mate = (grid, chip * 2 + 1 - core)
    across = [(grid, lax.rem(chip + j, chips) * 2 + core) for j in range(chips)]
    return chip, core, mate, across


def chip_barrier(mate, across):
    barrier = pltpu.get_barrier_semaphore()
    for peer in [mate] + across[1:]:
        pl.semaphore_signal(barrier, inc=1, device_id=peer, device_id_type=MESH)
    pl.semaphore_wait(barrier, len(across))


def send(src, dst, sems, peer):
    copy = pltpu.make_async_remote_copy(
        src_ref=src,
        dst_ref=dst,
        send_sem=sems[0],
        recv_sem=sems[1],
        device_id=peer,
        device_id_type=MESH,
    )
    copy.start()
    return copy


def gather_kernel(chips, x_ref, o_ref, far_s, far_r, mate_s, mate_r):
    chip, core, mate, across = chip_peers(chips)
    rows = x_ref.shape[0]
    parts = rows // STEP
    chip_barrier(mate, across)
    far, near = {}, {}
    base = (chip * 2 + core) * rows
    for q in range(parts):
        for j in range(1, chips):
            far[j, q] = send(
                x_ref.at[pl.ds(q * STEP, STEP)],
                o_ref.at[rows_at(base + q * STEP, STEP)],
                (far_s.at[j, q], far_r.at[j, q]),
                across[j],
            )
    for q in range(parts):
        near[0, q] = send(
            x_ref.at[pl.ds(q * STEP, STEP)],
            o_ref.at[rows_at(base + q * STEP, STEP)],
            (mate_s.at[0, q], mate_r.at[0, q]),
            mate,
        )
    o_ref[rows_at(base, rows), :] = x_ref[...]
    for q in range(parts):
        for j in range(1, chips):
            far[j, q].wait_recv()
            origin = (lax.rem(chip + chips - j, chips) * 2 + core) * rows + q * STEP
            block = o_ref.at[rows_at(origin, STEP)]
            near[j, q] = send(block, block, (mate_s.at[j, q], mate_r.at[j, q]), mate)
    for copy in near.values():
        copy.wait_recv()
    for copy in list(near.values()) + list(far.values()):
        copy.wait_send()


def cols_gather(value, collective_id):
    n = lax.axis_size("cols")
    chips, parts = n // 2, value.shape[0] // STEP
    sems = [pltpu.SemaphoreType.DMA((chips, parts))] * 4
    return pl.pallas_call(
        functools.partial(gather_kernel, chips),
        out_shape=jax.ShapeDtypeStruct((n * value.shape[0], value.shape[1]), jnp.float32),
        in_specs=[pl.BlockSpec(memory_space=pltpu.VMEM)],
        out_specs=pl.BlockSpec(memory_space=pltpu.VMEM),
        scratch_shapes=sems,
        compiler_params=pltpu.CompilerParams(
            collective_id=collective_id, has_side_effects=True, vmem_limit_bytes=12 << 20
        ),
    )(value)


def project_kernel(
    chips, u_ref, s_ref, o_ref, from_mate, to_far, from_far,
    a_s, a_r, b_s, b_r, c_s, c_r, d_s, d_r,
):
    chip, core, mate, across = chip_peers(chips)
    half = u_ref.shape[0] // 2
    part = half // chips
    pieces = part // STEP
    chip_barrier(mate, across)
    order = list(range(1, chips)) + [0]
    index = [lax.rem(chip + j, chips) * part for j in range(chips)]
    first, second, third, fourth = {}, {}, {}, {}
    for j in order:
        for q in range(pieces):
            first[j, q] = send(
                u_ref.at[rows_at((1 - core) * half + index[j] + q * STEP, STEP)],
                from_mate.at[j, q],
                (a_s.at[j, q], a_r.at[j, q]),
                mate,
            )
    for q in range(pieces):
        for j in range(1, chips):
            first[j, q].wait_recv()
            to_far[j, q] = u_ref[rows_at(core * half + index[j] + q * STEP, STEP), :] + from_mate[j, q]
            second[j, q] = send(
                to_far.at[j, q], from_far.at[j, q], (b_s.at[j, q], b_r.at[j, q]), across[j]
            )
    for q in range(pieces):
        mine = rows_at(core * half + index[0] + q * STEP, STEP)
        first[0, q].wait_recv()
        total = u_ref[mine, :] + from_mate[0, q]
        for j in range(1, chips):
            second[j, q].wait_recv()
            total = total + from_far[j, q]
        o_ref[mine, :] = s_ref[mine, :] - total
        for j in range(1, chips):
            third[j, q] = send(
                o_ref.at[mine], o_ref.at[mine], (c_s.at[j, q], c_r.at[j, q]), across[j]
            )
        fourth[0, q] = send(
            o_ref.at[mine], o_ref.at[mine], (d_s.at[0, q], d_r.at[0, q]), mate
        )
    for q in range(pieces):
        for j in range(1, chips):
            third[j, q].wait_recv()
            origin = core * half + lax.rem(chip + chips - j, chips) * part + q * STEP
            block = o_ref.at[rows_at(origin, STEP)]
            fourth[j, q] = send(block, block, (d_s.at[j, q], d_r.at[j, q]), mate)
    for copy in fourth.values():
        copy.wait_recv()
    for group in (first, second, third, fourth):
        for copy in group.values():
            copy.wait_send()


def project(combined, current, collective_id):
    chips = lax.axis_size("cols") // 2
    rows, width = combined.shape
    pieces = rows // 2 // chips // STEP
    slot = pltpu.VMEM((chips, pieces, STEP, width), jnp.float32)
    return pl.pallas_call(
        functools.partial(project_kernel, chips),
        out_shape=jax.ShapeDtypeStruct(combined.shape, jnp.float32),
        in_specs=[pl.BlockSpec(memory_space=pltpu.VMEM)] * 2,
        out_specs=pl.BlockSpec(memory_space=pltpu.VMEM),
        scratch_shapes=[slot] * 3 + [pltpu.SemaphoreType.DMA((chips, pieces))] * 8,
        compiler_params=pltpu.CompilerParams(
            collective_id=collective_id, has_side_effects=True, vmem_limit_bytes=24 << 20
        ),
    )(combined, current)


def shards(basis, snapshots, permittivity, labels, sigma_table):
    snap_cols = snapshots.shape[0]
    basis_cols = basis.shape[0]
    cell_shape = basis.shape[1:]
    grid_size = lax.axis_size("grid")
    total_snap = snap_cols * lax.axis_size("cols")
    unknowns = 3 * snapshots.shape[3] * snapshots.shape[2] * grid_size
    conductivity = lookup_sigma(labels, sigma_table)
    flat_basis = basis.reshape(basis_cols, -1)
    current = cols_gather(snapshots.reshape(snap_cols, -1), 1)
    coefficients = None
    for sweep_index in range(2):
        coef_part = grid_sum(cells_dot(flat_basis, current), 2 + sweep_index)
        combined = combine_rows(coef_part, flat_basis, HIGH if sweep_index else HIGHEST)
        current = project(combined, current, 4 + sweep_index)
        coefficients = coef_part if coefficients is None else coefficients + coef_part
    layers, layer = cell_shape[1], cell_shape[2]

    def layer_of(fields, component, at, count):
        start = (component * count + at) * layer
        return fields[:, start : start + layer]

    gram_sum = grid_sum(cells_dot(current, current), 6) / unknowns
    top = jnp.stack([layer_of(current, a, layers - 1, layers) for a in range(3)])
    bottom = jnp.stack([layer_of(current, a, 0, layers) for a in range(2)])
    gram_sum, top, bottom = lax.optimization_barrier((gram_sum, top, bottom))
    up = [(i, i + 1) for i in range(grid_size - 1)]
    down = [(j, i) for i, j in up]
    below = lax.ppermute(top, "grid", up)
    above = lax.ppermute(bottom, "grid", down)
    lower_factor = jnp.linalg.cholesky(gram_sum)
    identity = jnp.eye(total_snap, dtype=jnp.float32)
    inverse = jax.scipy.linalg.solve_triangular(lower_factor, identity, lower=True).T
    own_start = lax.axis_index("cols") * snap_cols
    new_all = combine_rows(inverse, current)
    mass_term = permittivity.reshape(1, -1) * new_all
    loss_term = jnp.tile(conductivity.reshape(1, -1), (1, 3)) * new_all
    mass_term, loss_term = lax.optimization_barrier((mass_term, loss_term))
    own_flat = lax.dynamic_slice_in_dim(new_all, own_start, snap_cols, 0)
    own_new = own_flat.reshape(snapshots.shape)
    new_below = [combine_rows(inverse, below[a]) for a in range(3)]
    new_above = [combine_rows(inverse, above[a]) for a in range(2)]
    extended = []
    for a in range(3):
        column = [new_below[a]]
        column += [layer_of(new_all, a, at, layers) for at in range(layers)]
        if a < 2:
            column.append(new_above[a])
        extended.append(column)
    curl_term = curl_curl(*extended, NY)
    pieces = [
        cells_dot(flat_basis, mass_term),
        cells_dot(flat_basis, loss_term),
        cells_dot(own_flat, mass_term) / unknowns,
        cells_dot(own_flat, loss_term) / unknowns,
        cells_dot(flat_basis, curl_term),
        cells_dot(own_flat, curl_term) / unknowns,
    ]
    terms = grid_sum(jnp.concatenate(pieces, axis=0), 7)
    starts = [0]
    for piece in pieces:
        starts.append(starts[-1] + piece.shape[0])
    parts = [terms[low:high] for low, high in zip(starts[:-1], starts[1:])]
    cross_terms = jnp.stack([parts[4], parts[0], parts[1]])
    block_terms = jnp.stack([parts[5], parts[2], parts[3]])
    return (own_new, coefficients, cross_terms, block_terms)


def solution(mesh):
    placed = (
        P("cols", None, "grid", None),
        P("cols", None, "grid", None),
        P(None, "grid", None),
        P("grid", None),
        P(),
    )
    return jax.shard_map(
        shards,
        mesh=mesh,
        in_specs=placed,
        out_specs=(
            P("cols", None, "grid", None),
            P("cols", None),
            P(None, "cols", None),
            P(None, "cols", None),
        ),
        check_vma=False,
    )
```

```python
import functools

import jax
import jax.numpy as jnp
from jax import lax
from jax.experimental import pallas as pl
from jax.experimental.pallas import tpu as pltpu
from jax.sharding import PartitionSpec as P

NY = 32


HIGHEST = lax.Precision.HIGHEST
HIGH = lax.Precision.HIGH
MESH = pl.DeviceIdType.MESH
STEP = 8


def cells_dot(left_rows, right_rows, precision=HIGH):
    left_flat = left_rows.reshape(left_rows.shape[0], -1)
    right_flat = right_rows.reshape(right_rows.shape[0], -1)
    return lax.dot_general(
        left_flat,
        right_flat,
        (((1,), (1,)), ((), ())),
        precision=precision,
        preferred_element_type=jnp.float32,
    )


def combine_rows(weights, fields, precision=HIGH):
    flattened = fields.reshape(fields.shape[0], -1)
    output_rows = lax.dot_general(
        weights,
        flattened,
        (((0,), (0,)), ((), ())),
        precision=precision,
        preferred_element_type=jnp.float32,
    )
    return output_rows.reshape((weights.shape[1],) + fields.shape[1:])


def forward_x(field, row_len):
    padding_cols = jnp.zeros(field.shape[:-1] + (row_len,), field.dtype)
    return jnp.concatenate([field[..., row_len:], padding_cols], axis=-1)


def backward_x(field, row_len):
    padding_cols = jnp.zeros(field.shape[:-1] + (row_len,), field.dtype)
    return jnp.concatenate([padding_cols, field[..., :-row_len]], axis=-1)


def forward_y(field, row_len):
    column_pos = lax.broadcasted_iota(jnp.int32, (field.shape[-1],), 0) % row_len
    padding_cols = jnp.zeros(field.shape[:-1] + (1,), field.dtype)
    shifted = jnp.concatenate([field[..., 1:], padding_cols], axis=-1)
    return jnp.where(column_pos != row_len - 1, shifted, 0.0)


def backward_y(field, row_len):
    column_pos = lax.broadcasted_iota(jnp.int32, (field.shape[-1],), 0) % row_len
    padding_cols = jnp.zeros(field.shape[:-1] + (1,), field.dtype)
    shifted = jnp.concatenate([padding_cols, field[..., :-1]], axis=-1)
    return jnp.where(column_pos != 0, shifted, 0.0)


def curl_curl(field_x, field_y, field_z, row_len):
    def plus_x(field):
        return forward_x(field, row_len) - field

    def minus_x(field):
        return field - backward_x(field, row_len)

    def plus_y(field):
        return forward_y(field, row_len) - field

    def minus_y(field):
        return field - backward_y(field, row_len)

    def second_x(field):
        return forward_x(field, row_len) - 2.0 * field + backward_x(field, row_len)

    def second_y(field):
        return forward_y(field, row_len) - 2.0 * field + backward_y(field, row_len)

    images = ([], [], [])
    for at in range(1, len(field_x) - 1):
        x_low, x_mid, x_top = field_x[at - 1 : at + 2]
        y_low, y_mid, y_top = field_y[at - 1 : at + 2]
        z_low, z_mid = field_z[at - 1 : at + 1]
        images[0].append(
            -second_y(x_mid)
            - (x_top - 2.0 * x_mid + x_low)
            + minus_y(plus_x(y_mid))
            + plus_x(z_mid - z_low)
        )
        images[1].append(
            -second_x(y_mid)
            - (y_top - 2.0 * y_mid + y_low)
            + minus_x(plus_y(x_mid))
            + plus_y(z_mid - z_low)
        )
        images[2].append(
            -second_x(z_mid) - second_y(z_mid) + minus_x(x_top - x_mid) + minus_y(y_top - y_mid)
        )
    return jnp.concatenate(images[0] + images[1] + images[2], axis=-1)


def lookup_sigma(labels, sigma_table):
    region_ids = jnp.arange(sigma_table.shape[0], dtype=jnp.int32)
    picked = jnp.where(labels[None] == region_ids[:, None, None], sigma_table[:, None, None], 0.0)
    return jnp.sum(picked, axis=0)


def rows_at(start, count):
    return pl.ds(pl.multiple_of(start, STEP), count)


def grid_sum_kernel(n, piece, x_ref, o_ref, slots, send_a, recv_a, send_b, recv_b):
    me = lax.axis_index("grid")
    col = lax.axis_index("cols")
    peers = [(lax.rem(me + k, n), col) for k in range(n)]
    barrier = pltpu.get_barrier_semaphore()
    for k in range(1, n):
        pl.semaphore_signal(barrier, inc=1, device_id=peers[k], device_id_type=MESH)
    pl.semaphore_wait(barrier, n - 1)
    scatter = {}
    for k in range(1, n):
        scatter[k] = pltpu.make_async_remote_copy(
            src_ref=x_ref.at[rows_at(peers[k][0] * piece, piece)],
            dst_ref=slots.at[k],
            send_sem=send_a.at[k],
            recv_sem=recv_a.at[k],
            device_id=peers[k],
            device_id_type=MESH,
        )
        scatter[k].start()
    mine = rows_at(me * piece, piece)
    total = x_ref[mine, :]
    for k in range(1, n):
        scatter[k].wait_recv()
        total = total + slots[k]
    o_ref[mine, :] = total
    spread = {}
    for k in range(1, n):
        spread[k] = pltpu.make_async_remote_copy(
            src_ref=o_ref.at[mine],
            dst_ref=o_ref.at[mine],
            send_sem=send_b.at[k],
            recv_sem=recv_b.at[k],
            device_id=peers[k],
            device_id_type=MESH,
        )
        spread[k].start()
    for k in range(1, n):
        spread[k].wait_recv()
    for k in range(1, n):
        scatter[k].wait_send()
        spread[k].wait_send()


def grid_sum(value, collective_id):
    n = lax.axis_size("grid")
    rows = value.shape[0]
    piece = -(-rows // (STEP * n)) * STEP
    padded_rows = piece * n
    if padded_rows != rows:
        value = jnp.pad(value, ((0, padded_rows - rows), (0, 0)))
    sems = [pltpu.SemaphoreType.DMA((n,))] * 4
    out = pl.pallas_call(
        functools.partial(grid_sum_kernel, n, piece),
        out_shape=jax.ShapeDtypeStruct(value.shape, jnp.float32),
        in_specs=[pl.BlockSpec(memory_space=pltpu.VMEM)],
        out_specs=pl.BlockSpec(memory_space=pltpu.VMEM),
        scratch_shapes=[pltpu.VMEM((n, piece, value.shape[1]), jnp.float32)] + sems,
        compiler_params=pltpu.CompilerParams(
            collective_id=collective_id, has_side_effects=True
        ),
    )(value)
    return out[:rows]


def chip_peers(chips):
    me = lax.axis_index("cols")
    grid = lax.axis_index("grid")
    chip, core = me // 2, lax.rem(me, 2)
    mate = (grid, chip * 2 + 1 - core)
    across = [(grid, lax.rem(chip + j, chips) * 2 + core) for j in range(chips)]
    return chip, core, mate, across


def chip_barrier(mate, across):
    barrier = pltpu.get_barrier_semaphore()
    for peer in [mate] + across[1:]:
        pl.semaphore_signal(barrier, inc=1, device_id=peer, device_id_type=MESH)
    pl.semaphore_wait(barrier, len(across))


def send(src, dst, sems, peer):
    copy = pltpu.make_async_remote_copy(
        src_ref=src,
        dst_ref=dst,
        send_sem=sems[0],
        recv_sem=sems[1],
        device_id=peer,
        device_id_type=MESH,
    )
    copy.start()
    return copy


def gather_kernel(chips, x_ref, o_ref, far_s, far_r, mate_s, mate_r):
    chip, core, mate, across = chip_peers(chips)
    rows = x_ref.shape[0]
    parts = rows // STEP
    chip_barrier(mate, across)
    far, near = {}, {}
    base = (chip * 2 + core) * rows
    for q in range(parts):
        for j in range(1, chips):
            far[j, q] = send(
                x_ref.at[pl.ds(q * STEP, STEP)],
                o_ref.at[rows_at(base + q * STEP, STEP)],
                (far_s.at[j, q], far_r.at[j, q]),
                across[j],
            )
    for q in range(parts):
        near[0, q] = send(
            x_ref.at[pl.ds(q * STEP, STEP)],
            o_ref.at[rows_at(base + q * STEP, STEP)],
            (mate_s.at[0, q], mate_r.at[0, q]),
            mate,
        )
    o_ref[rows_at(base, rows), :] = x_ref[...]
    for q in range(parts):
        for j in range(1, chips):
            far[j, q].wait_recv()
            origin = (lax.rem(chip + chips - j, chips) * 2 + core) * rows + q * STEP
            block = o_ref.at[rows_at(origin, STEP)]
            near[j, q] = send(block, block, (mate_s.at[j, q], mate_r.at[j, q]), mate)
    for copy in near.values():
        copy.wait_recv()
    for copy in list(near.values()) + list(far.values()):
        copy.wait_send()


def cols_gather(value, collective_id):
    n = lax.axis_size("cols")
    chips, parts = n // 2, value.shape[0] // STEP
    sems = [pltpu.SemaphoreType.DMA((chips, parts))] * 4
    return pl.pallas_call(
        functools.partial(gather_kernel, chips),
        out_shape=jax.ShapeDtypeStruct((n * value.shape[0], value.shape[1]), jnp.float32),
        in_specs=[pl.BlockSpec(memory_space=pltpu.VMEM)],
        out_specs=pl.BlockSpec(memory_space=pltpu.VMEM),
        scratch_shapes=sems,
        compiler_params=pltpu.CompilerParams(
            collective_id=collective_id, has_side_effects=True, vmem_limit_bytes=40 << 20
        ),
    )(value)


def project_kernel(
    chips, layers, u_ref, s_ref, o_ref, *refs
):
    edges = refs[: 2 if layers else 0]
    from_mate, to_far, from_far, a_s, a_r, b_s, b_r, c_s, c_r, d_s, d_r = refs[len(edges) :]
    chip, core, mate, across = chip_peers(chips)
    half = u_ref.shape[0] // 2
    part = half // chips
    pieces = part // STEP
    chip_barrier(mate, across)
    order = list(range(1, chips)) + [0]
    index = [lax.rem(chip + j, chips) * part for j in range(chips)]
    first, second, third, fourth = {}, {}, {}, {}
    for j in order:
        for q in range(pieces):
            first[j, q] = send(
                u_ref.at[rows_at((1 - core) * half + index[j] + q * STEP, STEP)],
                from_mate.at[j, q],
                (a_s.at[j, q], a_r.at[j, q]),
                mate,
            )
    for q in range(pieces):
        for j in range(1, chips):
            first[j, q].wait_recv()
            to_far[j, q] = u_ref[rows_at(core * half + index[j] + q * STEP, STEP), :] + from_mate[j, q]
            second[j, q] = send(
                to_far.at[j, q], from_far.at[j, q], (b_s.at[j, q], b_r.at[j, q]), across[j]
            )
    for q in range(pieces):
        mine = rows_at(core * half + index[0] + q * STEP, STEP)
        first[0, q].wait_recv()
        total = u_ref[mine, :] + from_mate[0, q]
        for j in range(1, chips):
            second[j, q].wait_recv()
            total = total + from_far[j, q]
        o_ref[mine, :] = s_ref[mine, :] - total
        for j in range(1, chips):
            third[j, q] = send(
                o_ref.at[mine], o_ref.at[mine], (c_s.at[j, q], c_r.at[j, q]), across[j]
            )
        fourth[0, q] = send(
            o_ref.at[mine], o_ref.at[mine], (d_s.at[0, q], d_r.at[0, q]), mate
        )
    for q in range(pieces):
        for j in range(1, chips):
            third[j, q].wait_recv()
            origin = core * half + lax.rem(chip + chips - j, chips) * part + q * STEP
            block = o_ref.at[rows_at(origin, STEP)]
            fourth[j, q] = send(block, block, (d_s.at[j, q], d_r.at[j, q]), mate)
    for copy in fourth.values():
        copy.wait_recv()
    if layers:
        top_ref, bottom_ref = edges
        layer = o_ref.shape[1] // 3 // layers
        for a in range(3):
            top_ref[:, a * layer : (a + 1) * layer] = o_ref[
                :, ((a + 1) * layers - 1) * layer : (a + 1) * layers * layer
            ]
        for a in range(2):
            bottom_ref[:, a * layer : (a + 1) * layer] = o_ref[
                :, a * layers * layer : (a * layers + 1) * layer
            ]
    for group in (first, second, third, fourth):
        for copy in group.values():
            copy.wait_send()


def project(combined, current, collective_id, layers=0):
    chips = lax.axis_size("cols") // 2
    rows, width = combined.shape
    pieces = rows // 2 // chips // STEP
    widths = [width]
    if layers:
        widths += [width // layers, width // 3 // layers * 2]
    slot = pltpu.VMEM((chips, pieces, STEP, width), jnp.float32)
    return pl.pallas_call(
        functools.partial(project_kernel, chips, layers),
        out_shape=[jax.ShapeDtypeStruct((rows, w), jnp.float32) for w in widths],
        in_specs=[pl.BlockSpec(memory_space=pltpu.VMEM)] * 2,
        out_specs=[pl.BlockSpec(memory_space=pltpu.VMEM)] * len(widths),
        scratch_shapes=[slot] * 3 + [pltpu.SemaphoreType.DMA((chips, pieces))] * 8,
        compiler_params=pltpu.CompilerParams(
            collective_id=collective_id, has_side_effects=True, vmem_limit_bytes=40 << 20
        ),
    )(combined, current)


def shards(basis, snapshots, permittivity, labels, sigma_table):
    snap_cols = snapshots.shape[0]
    basis_cols = basis.shape[0]
    cell_shape = basis.shape[1:]
    grid_size = lax.axis_size("grid")
    total_snap = snap_cols * lax.axis_size("cols")
    unknowns = 3 * snapshots.shape[3] * snapshots.shape[2] * grid_size
    conductivity = lookup_sigma(labels, sigma_table)
    flat_basis = basis.reshape(basis_cols, -1)
    current = cols_gather(snapshots.reshape(snap_cols, -1), 1)
    coefficients = None
    for sweep_index in range(2):
        coef_part = grid_sum(cells_dot(flat_basis, current), 2 + sweep_index)
        combined = combine_rows(coef_part, flat_basis, HIGH if sweep_index else HIGHEST)
        depth = cell_shape[1] if sweep_index else 0
        current, *edges = project(combined, current, 4 + sweep_index, depth)
        coefficients = coef_part if coefficients is None else coefficients + coef_part
    layers, layer = cell_shape[1], cell_shape[2]

    def layer_of(fields, component, at, count):
        start = (component * count + at) * layer
        return fields[:, start : start + layer]

    gram_sum = grid_sum(cells_dot(current, current), 6) / unknowns
    top, bottom = edges
    gram_sum, top, bottom = lax.optimization_barrier((gram_sum, top, bottom))
    up = [(i, i + 1) for i in range(grid_size - 1)]
    down = [(j, i) for i, j in up]
    below = lax.ppermute(top, "grid", up)
    above = lax.ppermute(bottom, "grid", down)
    lower_factor = jnp.linalg.cholesky(gram_sum)
    identity = jnp.eye(total_snap, dtype=jnp.float32)
    inverse = jax.scipy.linalg.solve_triangular(lower_factor, identity, lower=True).T
    own_start = lax.axis_index("cols") * snap_cols
    new_all = combine_rows(inverse, current)
    mass_term = permittivity.reshape(1, -1) * new_all
    loss_term = jnp.tile(conductivity.reshape(1, -1), (1, 3)) * new_all
    own_flat = lax.dynamic_slice_in_dim(new_all, own_start, snap_cols, 0)
    own_new = own_flat.reshape(snapshots.shape)
    new_below = combine_rows(inverse, below)
    new_above = combine_rows(inverse, above)
    extended = []
    for a in range(3):
        column = [layer_of(new_below, a, 0, 1)]
        column += [layer_of(new_all, a, at, layers) for at in range(layers)]
        if a < 2:
            column.append(layer_of(new_above, a, 0, 1))
        extended.append(column)
    curl_term = curl_curl(*extended, NY)
    pair = jnp.concatenate([mass_term, loss_term], axis=0)
    basis_pair = cells_dot(flat_basis, pair)
    own_pair = cells_dot(own_flat, pair) / unknowns
    pieces = [
        basis_pair[:, :total_snap],
        basis_pair[:, total_snap:],
        own_pair[:, :total_snap],
        own_pair[:, total_snap:],
        cells_dot(flat_basis, curl_term),
        cells_dot(own_flat, curl_term) / unknowns,
    ]
    terms = grid_sum(jnp.concatenate(pieces, axis=0), 7)
    starts = [0]
    for piece in pieces:
        starts.append(starts[-1] + piece.shape[0])
    parts = [terms[low:high] for low, high in zip(starts[:-1], starts[1:])]
    cross_terms = jnp.stack([parts[4], parts[0], parts[1]])
    block_terms = jnp.stack([parts[5], parts[2], parts[3]])
    return (own_new, coefficients, cross_terms, block_terms)


def solution(mesh):
    placed = (
        P("cols", None, "grid", None),
        P("cols", None, "grid", None),
        P(None, "grid", None),
        P("grid", None),
        P(),
    )
    return jax.shard_map(
        shards,
        mesh=mesh,
        in_specs=placed,
        out_specs=(
            P("cols", None, "grid", None),
            P("cols", None),
            P(None, "cols", None),
            P(None, "cols", None),
        ),
        check_vma=False,
    )
```
